32 devices in a mesh: grp: 2 (over y), hid: 4 (over z), feat: 4 (over x, core).
Axes of the slice: x: 2, y: 2, z: 4, core: 2. Of those that a mesh axis runs over, the one named last changes fastest.
Arguments:
- tokens: bfloat16 [128, 8192], P(('grp', 'hid'), 'feat'), parts along dimension 0, may hold values from -6 to 6
- gate_weight: bfloat16 [8192, 16384], P('feat', 'hid'), may hold values from -0.0625 to 0.0625
- up_weight: bfloat16 [8192, 16384], P('feat', 'hid'), may hold values from -0.0625 to 0.0625
- down_weight: bfloat16 [16384, 8192], P('hid', 'feat'), may hold values from -0.046875 to 0.046875
Outputs:
- mixed: bfloat16 [128, 8192], P(('grp', 'hid'), 'feat'), parts along dimension 0
The draws below stay inside these ranges and needn't reach their ends.
There are 2 independent parts, one for each index of `grp`. The reference program is written for one: setup_inputs(seed, part) draws one part's arguments, and reference() takes and returns one part's arrays. A program takes and returns all parts, laid end to end along the dimension named above; an argument that names none is the same for every part. Nothing has to cross between parts.
All inputs are finite; a program needn't handle non-finite values.
Results may differ from the reference program's by a relative error of at most 0.02.
Values may be sent and summed in bfloat16 or wider, within the bound.
A program may use at most 128 MiB of HBM per device.

```python
import jax
import jax.numpy as jnp
from jax import lax

D = 8192
FF = 16384
BATCH = 64
N_HID = 4
N_FEAT = 4


def steps_of(key, extent, shards, low, high):
    loudness, own = 1.0, jax.random.fold_in(key, 6)
    for position, parts in shards:
        heights = jnp.exp(jax.random.uniform(jax.random.fold_in(own, position), (parts,), jnp.float32, low / len(shards), high / len(shards)))
        loudness = loudness * jnp.repeat(heights, extent[position] // parts).reshape([-1 if axis == position else 1 for axis in range(len(extent))])
    return loudness


def gaussian(key, dims, spread, bound, split=(), dtype=jnp.bfloat16):
    loudness = steps_of(key, dims, split, -0.22, 0.18) if split else 1.0
    drawn = jax.random.normal(key, dims, jnp.float32) * spread * loudness
    return jnp.minimum(jnp.maximum(drawn, -bound), bound).astype(dtype)


def setup_inputs(seed: int = 0, part: int = 0) -> dict:
    splits = jax.random.split(jax.random.key(seed), 5)
    part_splits = jax.random.split(jax.random.fold_in(splits[4], part), 5)
    return {
        "tokens": gaussian(part_splits[0], (BATCH, D), 1.0, 6.0, ((0, 4), (1, 4))),
        "gate_weight": gaussian(splits[1], (D, FF), D ** -0.5, 0.0625, ((0, 4), (1, 4))),
        "up_weight": gaussian(splits[2], (D, FF), D ** -0.5, 0.0625, ((0, 4), (1, 4))),
        "down_weight": gaussian(splits[3], (FF, D), FF ** -0.5, 0.046875, ((0, 4), (1, 4))),
    }


def reference(tokens, gate_weight, up_weight, down_weight):
    feat_width = D // N_FEAT
    hid_width = FF // N_HID

    def feat_step(block_index, carry):
        gate_sum, up_sum = carry
        offset = (block_index * feat_width).astype(jnp.int32)
        row_block = lax.dynamic_slice_in_dim(tokens, offset, feat_width, 1)
        gate_part = jnp.dot(row_block, lax.dynamic_slice_in_dim(gate_weight, offset, feat_width, 0), preferred_element_type=jnp.float32)
        up_part = jnp.dot(row_block, lax.dynamic_slice_in_dim(up_weight, offset, feat_width, 0), preferred_element_type=jnp.float32)
        gate_part = lax.optimization_barrier(gate_part.astype(jnp.bfloat16)).astype(jnp.float32)
        up_part = lax.optimization_barrier(up_part.astype(jnp.bfloat16)).astype(jnp.float32)
        return gate_sum + gate_part, up_sum + up_part

    zeros = jnp.zeros((tokens.shape[0], FF), jnp.float32)
    gate_sum, up_sum = lax.fori_loop(0, N_FEAT, feat_step, (zeros, zeros))
    hidden = (jax.nn.silu(gate_sum) * up_sum).astype(jnp.bfloat16)

    def hid_step(block_index, total):
        offset = (block_index * hid_width).astype(jnp.int32)
        columns = lax.dynamic_slice_in_dim(hidden, offset, hid_width, 1)
        weights = lax.dynamic_slice_in_dim(down_weight, offset, hid_width, 0)
        partial_sum = jnp.dot(columns, weights, preferred_element_type=jnp.float32)
        return total + lax.optimization_barrier(partial_sum.astype(jnp.bfloat16)).astype(jnp.float32)

    mixed = lax.fori_loop(0, N_HID, hid_step, jnp.zeros((tokens.shape[0], D), jnp.float32))
    return mixed.astype(jnp.bfloat16)
```

```python
import functools

import jax
import jax.numpy as jnp
from jax import lax
from jax.experimental import pallas as pl
from jax.experimental.pallas import tpu as pltpu
from jax.sharding import PartitionSpec as P

MESH = pl.DeviceIdType.MESH
F32, BF16 = jnp.float32, jnp.bfloat16


def each(count, body):
    if count <= 4:
        for i in range(count):
            body(i)
    else:
        lax.fori_loop(0, count, lambda i, _: (body(i), 0)[1], 0)


def kernel(
    H, X, tok_ref, gate_ref, up_ref, down_ref, out_ref,
    tok, wg, wu, wd, part, pair_in, x_out, x_in, hid, o_part, o_in,
    wg_sem, wu_sem, wd_sem, own_sem, tok_s, tok_r, pair_s, pair_r, x_s, x_r,
    hp_s, hp_r, hx_s, hx_r, hf_s, hf_r, o_s, o_r,
):
    nch, _, cn = wg.shape
    nd, _, dn = wd.shape
    F = 2 * X
    rf = part.shape[3]
    r_in = tok.shape[1]
    rows = H * r_in
    ob = max(2, min(F, 256 // rf))
    block = ob * rf

    h = lax.axis_index("hid")
    f = lax.axis_index("feat")
    x, c = lax.div(f, 2), lax.rem(f, 2)
    pair = {"feat": x * 2 + 1 - c}

    def x_peer(d):
        return lax.rem(x + d, X)

    def remote(src, dst, ssem, rsem, device):
        return pltpu.make_async_remote_copy(
            src_ref=src, dst_ref=dst, send_sem=ssem, recv_sem=rsem,
            device_id=device, device_id_type=MESH,
        )

    def cols(ref, k, n):
        return ref.at[:, pl.ds(pl.multiple_of(k * n, n), n)]

    def wg_copy(k):
        return pltpu.make_async_copy(cols(gate_ref, k, cn), wg.at[k], wg_sem.at[k])

    def wu_copy(k):
        return pltpu.make_async_copy(cols(up_ref, k, cn), wu.at[k], wu_sem.at[k])

    def wd_copy(n):
        return pltpu.make_async_copy(cols(down_ref, n, dn), wd.at[n], wd_sem.at[n])

    def tok_copy(d):
        to = lax.rem(h + d + 1, H)
        return remote(tok_ref, tok.at[h], tok_s.at[d], tok_r.at[d], {"hid": to})

    def pair_copy(k):
        return remote(part.at[k, :, 1 - c], pair_in.at[k], pair_s.at[k], pair_r.at[k], pair)

    def x_copy(k, d):
        to = {"feat": x_peer(d + 1) * 2 + c}
        return remote(x_out.at[k, d], x_in.at[k, d], x_s.at[k, d], x_r.at[k, d], to)

    def hp_copy(k):
        return remote(hid.at[k, f], hid.at[k, f], hp_s.at[k], hp_r.at[k], pair)

    def hx_copy(k, d):
        to = {"feat": x_peer(d + 1) * 2 + c}
        return remote(hid.at[k, f], hid.at[k, f], hx_s.at[k, d], hx_r.at[k, d], to)

    def hf_copy(k, d):
        owner = lax.rem(x + X - d - 1, X) * 2 + c
        piece = hid.at[k, owner]
        return remote(piece, piece, hf_s.at[k, d], hf_r.at[k, d], pair)

    def o_copy(n, d):
        to = lax.rem(h + d + 1, H)
        return remote(o_part.at[n, to], o_in.at[n, d], o_s.at[n, d], o_r.at[n, d], {"hid": to})

    own_copy = pltpu.make_async_copy(tok_ref, tok.at[h], own_sem)
    own_copy.start()

    barrier = pltpu.get_barrier_semaphore()
    each(H - 1, lambda d: pl.semaphore_signal(
        barrier, inc=1, device_id={"hid": lax.rem(h + d + 1, H)}, device_id_type=MESH))
    each(X - 1, lambda d: pl.semaphore_signal(
        barrier, inc=1, device_id={"feat": x_peer(d + 1) * 2 + c}, device_id_type=MESH))
    pl.semaphore_signal(barrier, inc=1, device_id=pair, device_id_type=MESH)

    def start_gate_up(k):
        wg_copy(k).start()
        wu_copy(k).start()

    each(nch, start_gate_up)
    each(nd, lambda n: wd_copy(n).start())
    pl.semaphore_wait(barrier, H - 1 + X)

    each(H - 1, lambda d: tok_copy(d).start())
    own_copy.wait()
    each(H - 1, lambda d: tok_copy(d).wait_recv())

    def multiply(k):
        wg_copy(k).wait()
        wu_copy(k).wait()
        for j in range(rows // block):
            held = block // r_in
            lhs = tok[j * held:(j + 1) * held].reshape(block, tok.shape[2])
            for w, base in ((wg, 0), (wu, cn)):
                got = jnp.dot(lhs, w[k], preferred_element_type=F32).astype(BF16)
                got = got.reshape(ob // 2, 2, rf, cn)
                part[k, j * (ob // 2):(j + 1) * (ob // 2), :, :, base:base + cn] = got
        pair_copy(k).start()

    def across(k):
        pair_copy(k).wait_recv()

        def send(d):
            to = x_peer(d + 1)
            summed = part[k, to, c].astype(F32) + pair_in[k, to].astype(F32)
            x_out[k, d] = summed.astype(BF16)
            x_copy(k, d).start()

        each(X - 1, send)

    def activate(k):
        total = part[k, x, c].astype(F32) + pair_in[k, x].astype(F32)
        for d in range(X - 1):
            x_copy(k, d).wait_recv()
            total = total + x_in[k, d].astype(F32)
        gate, up = total[:, :cn], total[:, cn:]
        hid[k, f] = (gate / (1.0 + jnp.exp(-gate)) * up).astype(BF16)
        each(X - 1, lambda d: hx_copy(k, d).start())
        hp_copy(k).start()

    def forward(k):
        def step(d):
            hx_copy(k, d).wait_recv()
            hf_copy(k, d).start()

        each(X - 1, step)

    stages = (multiply, across, activate, forward)

    def turn(t, _):
        for lag, stage in enumerate(stages):
            k = t - lag

            @pl.when(jnp.logical_and(k >= 0, k < nch))
            def _():
                stage(k)

        return 0

    lax.fori_loop(0, nch + len(stages) - 1, turn, 0)

    def arrived(k):
        hp_copy(k).wait_recv()
        each(X - 1, lambda d: hf_copy(k, d).wait_recv())

    each(nch, arrived)

    def project(n, _):
        wd_copy(n).wait()
        for j in range(rows // block):
            first = j * ob
            lhs = jnp.concatenate(
                [hid[k, first:first + ob].reshape(block, cn) for k in range(nch)], axis=1)
            got = jnp.dot(lhs, wd[n], preferred_element_type=F32).astype(BF16)
            held = block // r_in
            o_part[n, j * held:(j + 1) * held] = got.reshape(held, r_in, dn)
        each(H - 1, lambda d: o_copy(n, d).start())
        return 0

    lax.fori_loop(0, nd, project, 0)

    for n in range(nd):
        each(H - 1, lambda d: o_copy(n, d).wait_recv())
        total = o_part[n, h].astype(F32)
        for d in range(H - 1):
            total = total + o_in[n, d].astype(F32)
        out_ref[:, n * dn:(n + 1) * dn] = total.astype(BF16)

    each(H - 1, lambda d: tok_copy(d).wait_send())

    def sent(k):
        pair_copy(k).wait_send()
        hp_copy(k).wait_send()

        def over(d):
            x_copy(k, d).wait_send()
            hx_copy(k, d).wait_send()
            hf_copy(k, d).wait_send()

        each(X - 1, over)

    each(nch, sent)
    each(nd, lambda n: each(H - 1, lambda d: o_copy(n, d).wait_send()))


def shards(H, F, tokens, gate_weight, up_weight, down_weight):
    r_in, k1 = tokens.shape
    n1 = gate_weight.shape[1]
    k2, n2 = down_weight.shape
    X = F // 2
    rf = r_in * H // F
    cn = min(512, n1)
    dn = min(256, n2)
    nch, nd = n1 // cn, n2 // dn
    dma = lambda *dims: pltpu.SemaphoreType.DMA(dims)
    buf = lambda *dims: pltpu.VMEM(dims, BF16)
    return pl.pallas_call(
        functools.partial(kernel, H, X),
        out_shape=jax.ShapeDtypeStruct((r_in, n2), BF16),
        in_specs=[pl.BlockSpec(memory_space=pl.ANY)] * 4,
        out_specs=pl.BlockSpec(memory_space=pltpu.VMEM),
        scratch_shapes=[
            buf(H, r_in, k1),
            buf(nch, k1, cn), buf(nch, k1, cn), buf(nd, k2, dn),
            buf(nch, X, 2, rf, 2 * cn), buf(nch, X, rf, 2 * cn),
            buf(nch, X - 1, rf, 2 * cn), buf(nch, X - 1, rf, 2 * cn),
            buf(nch, F, rf, cn),
            buf(nd, H, r_in, dn), buf(nd, H - 1, r_in, dn),
            dma(nch), dma(nch), dma(nd), pltpu.SemaphoreType.DMA,
            dma(H - 1), dma(H - 1),
            dma(nch), dma(nch), dma(nch, X - 1), dma(nch, X - 1),
            dma(nch), dma(nch), dma(nch, X - 1), dma(nch, X - 1),
            dma(nch, X - 1), dma(nch, X - 1),
            dma(nd, H - 1), dma(nd, H - 1),
        ],
        compiler_params=pltpu.CompilerParams(
            collective_id=0, has_side_effects=True, vmem_limit_bytes=60 * 2**20),
    )(tokens, gate_weight, up_weight, down_weight)


def solution(mesh):
    placed = (P(("grp", "hid"), "feat"), P("feat", "hid"), P("feat", "hid"), P("hid", "feat"))
    return jax.shard_map(
        functools.partial(shards, mesh.shape["hid"], mesh.shape["feat"]),
        mesh=mesh, in_specs=placed, out_specs=P(("grp", "hid"), "feat"), check_vma=False,
    )
```

```python
import functools

import jax
import jax.numpy as jnp
from jax import lax
from jax.experimental import pallas as pl
from jax.experimental.pallas import tpu as pltpu
from jax.sharding import PartitionSpec as P

MESH = pl.DeviceIdType.MESH
F32, BF16 = jnp.float32, jnp.bfloat16


def each(count, body):
    if count <= 4:
        for i in range(count):
            body(i)
    else:
        lax.fori_loop(0, count, lambda i, _: (body(i), 0)[1], 0)


def kernel(
    H, X, tok_ref, gate_ref, up_ref, down_ref, out_ref,
    tok, wg, wu, wd, part, pair_in, x_out, x_in, hid, o_part, o_in,
    wg_sem, wu_sem, wd_sem, own_sem, tok_s, tok_r, pair_s, pair_r, x_s, x_r,
    hp_s, hp_r, hx_s, hx_r, hf_s, hf_r, o_s, o_r,
):
    nch, _, cn = wg.shape
    nd, _, dn = wd.shape
    F = 2 * X
    rf = part.shape[3]
    r_in = tok.shape[1]
    rows = H * r_in
    ob = max(2, min(F, 256 // rf))
    block = ob * rf

    h = lax.axis_index("hid")
    f = lax.axis_index("feat")
    x, c = lax.div(f, 2), lax.rem(f, 2)
    pair = {"feat": x * 2 + 1 - c}

    def x_peer(d):
        return lax.rem(x + d, X)

    def remote(src, dst, ssem, rsem, device):
        return pltpu.make_async_remote_copy(
            src_ref=src, dst_ref=dst, send_sem=ssem, recv_sem=rsem,
            device_id=device, device_id_type=MESH,
        )

    def cols(ref, k, n):
        return ref.at[:, pl.ds(pl.multiple_of(k * n, n), n)]

    def wg_copy(k):
        return pltpu.make_async_copy(cols(gate_ref, k, cn), wg.at[k], wg_sem.at[k])

    def wu_copy(k):
        return pltpu.make_async_copy(cols(up_ref, k, cn), wu.at[k], wu_sem.at[k])

    def wd_copy(n):
        return pltpu.make_async_copy(cols(down_ref, n, dn), wd.at[n], wd_sem.at[n])

    def tok_copy(d):
        to = lax.rem(h + d + 1, H)
        return remote(tok_ref, tok.at[h], tok_s.at[d], tok_r.at[d], {"hid": to})

    def pair_copy(k):
        return remote(part.at[k, :, 1 - c], pair_in.at[k], pair_s.at[k], pair_r.at[k], pair)

    def x_copy(k, d):
        to = {"feat": x_peer(d + 1) * 2 + c}
        return remote(x_out.at[k, d], x_in.at[k, d], x_s.at[k, d], x_r.at[k, d], to)

    def hp_copy(k):
        return remote(hid.at[k, f], hid.at[k, f], hp_s.at[k], hp_r.at[k], pair)

    def hx_copy(k, d):
        to = {"feat": x_peer(d + 1) * 2 + c}
        return remote(hid.at[k, f], hid.at[k, f], hx_s.at[k, d], hx_r.at[k, d], to)

    def hf_copy(k, d):
        owner = lax.rem(x + X - d - 1, X) * 2 + c
        piece = hid.at[k, owner]
        return remote(piece, piece, hf_s.at[k, d], hf_r.at[k, d], pair)

    def o_copy(n, d):
        to = lax.rem(h + d + 1, H)
        return remote(o_part.at[n, to], o_in.at[n, d], o_s.at[n, d], o_r.at[n, d], {"hid": to})

    own_copy = pltpu.make_async_copy(tok_ref, tok.at[h], own_sem)
    own_copy.start()

    barrier = pltpu.get_barrier_semaphore()
    each(H - 1, lambda d: pl.semaphore_signal(
        barrier, inc=1, device_id={"hid": lax.rem(h + d + 1, H)}, device_id_type=MESH))
    each(X - 1, lambda d: pl.semaphore_signal(
        barrier, inc=1, device_id={"feat": x_peer(d + 1) * 2 + c}, device_id_type=MESH))
    pl.semaphore_signal(barrier, inc=1, device_id=pair, device_id_type=MESH)

    def start_gate_up(k):
        wg_copy(k).start()
        wu_copy(k).start()

    each(nch, start_gate_up)
    each(nd, lambda n: wd_copy(n).start())
    pl.semaphore_wait(barrier, H - 1 + X)

    each(H - 1, lambda d: tok_copy(d).start())
    own_copy.wait()
    each(H - 1, lambda d: tok_copy(d).wait_recv())

    def multiply(k):
        wg_copy(k).wait()
        wu_copy(k).wait()
        for j in range(rows // block):
            held = block // r_in
            lhs = tok[j * held:(j + 1) * held].reshape(block, tok.shape[2])
            for w, base in ((wg, 0), (wu, cn)):
                got = jnp.dot(lhs, w[k], preferred_element_type=F32).astype(BF16)
                got = got.reshape(ob // 2, 2, rf, cn)
                part[k, j * (ob // 2):(j + 1) * (ob // 2), :, :, base:base + cn] = got
        pair_copy(k).start()

    def across(k):
        pair_copy(k).wait_recv()

        def send(d):
            to = x_peer(d + 1)
            summed = part[k, to, c].astype(F32) + pair_in[k, to].astype(F32)
            x_out[k, d] = summed.astype(BF16)
            x_copy(k, d).start()

        each(X - 1, send)

    def activate(k):
        total = part[k, x, c].astype(F32) + pair_in[k, x].astype(F32)
        for d in range(X - 1):
            x_copy(k, d).wait_recv()
            total = total + x_in[k, d].astype(F32)
        gate, up = total[:, :cn], total[:, cn:]
        hid[k, f] = (gate / (1.0 + jnp.exp(-gate)) * up).astype(BF16)
        each(X - 1, lambda d: hx_copy(k, d).start())
        hp_copy(k).start()

    def forward(k):
        def step(d):
            hx_copy(k, d).wait_recv()
            hf_copy(k, d).start()

        each(X - 1, step)

    stages = ((0, multiply), (1, across), (5, activate), (9, forward))

    def turn(t, _):
        for lag, stage in stages:
            k = t - lag

            @pl.when(jnp.logical_and(k >= 0, k < nch))
            def _():
                stage(k)

        return 0

    lax.fori_loop(0, nch + stages[-1][0], turn, 0)

    def arrived(k):
        hp_copy(k).wait_recv()
        each(X - 1, lambda d: hf_copy(k, d).wait_recv())

    each(nch, arrived)

    def project(n, _):
        wd_copy(n).wait()
        for j in range(rows // block):
            first = j * ob
            lhs = jnp.concatenate(
                [hid[k, first:first + ob].reshape(block, cn) for k in range(nch)], axis=1)
            got = jnp.dot(lhs, wd[n], preferred_element_type=F32).astype(BF16)
            held = block // r_in
            o_part[n, j * held:(j + 1) * held] = got.reshape(held, r_in, dn)
        each(H - 1, lambda d: o_copy(n, d).start())
        return 0

    lax.fori_loop(0, nd, project, 0)

    for n in range(nd):
        each(H - 1, lambda d: o_copy(n, d).wait_recv())
        total = o_part[n, h].astype(F32)
        for d in range(H - 1):
            total = total + o_in[n, d].astype(F32)
        out_ref[:, n * dn:(n + 1) * dn] = total.astype(BF16)

    each(H - 1, lambda d: tok_copy(d).wait_send())

    def sent(k):
        pair_copy(k).wait_send()
        hp_copy(k).wait_send()

        def over(d):
            x_copy(k, d).wait_send()
            hx_copy(k, d).wait_send()
            hf_copy(k, d).wait_send()

        each(X - 1, over)

    each(nch, sent)
    each(nd, lambda n: each(H - 1, lambda d: o_copy(n, d).wait_send()))


def shards(H, F, tokens, gate_weight, up_weight, down_weight):
    r_in, k1 = tokens.shape
    n1 = gate_weight.shape[1]
    k2, n2 = down_weight.shape
    X = F // 2
    rf = r_in * H // F
    cn = min(512, n1)
    dn = min(512, n2)
    nch, nd = n1 // cn, n2 // dn
    dma = lambda *dims: pltpu.SemaphoreType.DMA(dims)
    buf = lambda *dims: pltpu.VMEM(dims, BF16)
    return pl.pallas_call(
        functools.partial(kernel, H, X),
        out_shape=jax.ShapeDtypeStruct((r_in, n2), BF16),
        in_specs=[pl.BlockSpec(memory_space=pl.ANY)] * 4,
        out_specs=pl.BlockSpec(memory_space=pltpu.VMEM),
        scratch_shapes=[
            buf(H, r_in, k1),
            buf(nch, k1, cn), buf(nch, k1, cn), buf(nd, k2, dn),
            buf(nch, X, 2, rf, 2 * cn), buf(nch, X, rf, 2 * cn),
            buf(nch, X - 1, rf, 2 * cn), buf(nch, X - 1, rf, 2 * cn),
            buf(nch, F, rf, cn),
            buf(nd, H, r_in, dn), buf(nd, H - 1, r_in, dn),
            dma(nch), dma(nch), dma(nd), pltpu.SemaphoreType.DMA,
            dma(H - 1), dma(H - 1),
            dma(nch), dma(nch), dma(nch, X - 1), dma(nch, X - 1),
            dma(nch), dma(nch), dma(nch, X - 1), dma(nch, X - 1),
            dma(nch, X - 1), dma(nch, X - 1),
            dma(nd, H - 1), dma(nd, H - 1),
        ],
        compiler_params=pltpu.CompilerParams(
            collective_id=0, has_side_effects=True, vmem_limit_bytes=60 * 2**20),
    )(tokens, gate_weight, up_weight, down_weight)


def solution(mesh):
    placed = (P(("grp", "hid"), "feat"), P("feat", "hid"), P("feat", "hid"), P("hid", "feat"))
    return jax.shard_map(
        functools.partial(shards, mesh.shape["hid"], mesh.shape["feat"]),
        mesh=mesh, in_specs=placed, out_specs=P(("grp", "hid"), "feat"), check_vma=False,
    )
```

```python
import functools

import jax
import jax.numpy as jnp
from jax import lax
from jax.experimental import pallas as pl
from jax.experimental.pallas import tpu as pltpu
from jax.sharding import PartitionSpec as P

MESH = pl.DeviceIdType.MESH
F32, BF16 = jnp.float32, jnp.bfloat16
X_LAG, H_LAG, D_LAG = 4, 7, 8


def each(count, body):
    if count <= 4:
        for i in range(count):
            body(i)
    else:
        lax.fori_loop(0, count, lambda i, _: (body(i), 0)[1], 0)


def kernel(
    H, X, tok_ref, gate_ref, up_ref, down_ref, out_ref,
    tok, wg, wu, wd, part, pair_in, x_out, x_in, hid, acc, o_part, o_in,
    wg_sem, wu_sem, wd_sem, own_sem, tok_s, tok_r, pair_s, pair_r, x_s, x_r,
    hp_s, hp_r, hx_s, hx_r, hf_s, hf_r, o_s, o_r,
):
    nch, _, cn = wg.shape
    nd, _, _, dn = o_part.shape
    F = 2 * X
    rf = part.shape[3]
    r_in = tok.shape[1]
    rows = H * r_in
    ob = max(2, min(F, 256 // rf))
    block = ob * rf

    h = lax.axis_index("hid")
    f = lax.axis_index("feat")
    x, c = lax.div(f, 2), lax.rem(f, 2)
    pair = {"feat": x * 2 + 1 - c}

    def x_peer(d):
        return lax.rem(x + d, X)

    def remote(src, dst, ssem, rsem, device):
        return pltpu.make_async_remote_copy(
            src_ref=src, dst_ref=dst, send_sem=ssem, recv_sem=rsem,
            device_id=device, device_id_type=MESH,
        )

    def cols(ref, k, n):
        return ref.at[:, pl.ds(pl.multiple_of(k * n, n), n)]

    def wg_copy(k):
        return pltpu.make_async_copy(cols(gate_ref, k, cn), wg.at[k], wg_sem.at[k])

    def wu_copy(k):
        return pltpu.make_async_copy(cols(up_ref, k, cn), wu.at[k], wu_sem.at[k])

    def wd_copy(k):
        rows_k = pl.ds(pl.multiple_of(k * cn, cn), cn)
        return pltpu.make_async_copy(down_ref.at[rows_k], wd.at[k], wd_sem.at[k])

    def tok_copy(d):
        to = lax.rem(h + d + 1, H)
        return remote(tok_ref, tok.at[h], tok_s.at[d], tok_r.at[d], {"hid": to})

    def pair_copy(k):
        return remote(part.at[k, :, 1 - c], pair_in.at[k], pair_s.at[k], pair_r.at[k], pair)

    def x_copy(k, d):
        to = {"feat": x_peer(d + 1) * 2 + c}
        return remote(x_out.at[k, d], x_in.at[k, d], x_s.at[k, d], x_r.at[k, d], to)

    def hp_copy(k):
        return remote(hid.at[k, f], hid.at[k, f], hp_s.at[k], hp_r.at[k], pair)

    def hx_copy(k, d):
        to = {"feat": x_peer(d + 1) * 2 + c}
        return remote(hid.at[k, f], hid.at[k, f], hx_s.at[k, d], hx_r.at[k, d], to)

    def hf_copy(k, d):
        owner = lax.rem(x + X - d - 1, X) * 2 + c
        piece = hid.at[k, owner]
        return remote(piece, piece, hf_s.at[k, d], hf_r.at[k, d], pair)

    def o_copy(n, d):
        to = lax.rem(h + d + 1, H)
        return remote(o_part.at[n, to], o_in.at[n, d], o_s.at[n, d], o_r.at[n, d], {"hid": to})

    own_copy = pltpu.make_async_copy(tok_ref, tok.at[h], own_sem)
    own_copy.start()

    barrier = pltpu.get_barrier_semaphore()
    each(H - 1, lambda d: pl.semaphore_signal(
        barrier, inc=1, device_id={"hid": lax.rem(h + d + 1, H)}, device_id_type=MESH))
    each(X - 1, lambda d: pl.semaphore_signal(
        barrier, inc=1, device_id={"feat": x_peer(d + 1) * 2 + c}, device_id_type=MESH))
    pl.semaphore_signal(barrier, inc=1, device_id=pair, device_id_type=MESH)

    def start_gate_up(k):
        wg_copy(k).start()
        wu_copy(k).start()

    each(nch, start_gate_up)
    each(nch, lambda k: wd_copy(k).start())
    acc[...] = jnp.zeros_like(acc)
    pl.semaphore_wait(barrier, H - 1 + X)

    each(H - 1, lambda d: tok_copy(d).start())
    own_copy.wait()
    each(H - 1, lambda d: tok_copy(d).wait_recv())

    def multiply(k):
        wg_copy(k).wait()
        wu_copy(k).wait()
        for j in range(rows // block):
            held = block // r_in
            lhs = tok[j * held:(j + 1) * held].reshape(block, tok.shape[2])
            for w, base in ((wg, 0), (wu, cn)):
                got = jnp.dot(lhs, w[k], preferred_element_type=F32).astype(BF16)
                got = got.reshape(ob // 2, 2, rf, cn)
                part[k, j * (ob // 2):(j + 1) * (ob // 2), :, :, base:base + cn] = got
        pair_copy(k).start()

    def across(k):
        pair_copy(k).wait_recv()

        def send(d):
            to = x_peer(d + 1)
            summed = part[k, to, c].astype(F32) + pair_in[k, to].astype(F32)
            x_out[k, d] = summed.astype(BF16)
            x_copy(k, d).start()

        each(X - 1, send)

    def activate(k):
        total = part[k, x, c].astype(F32) + pair_in[k, x].astype(F32)
        for d in range(X - 1):
            x_copy(k, d).wait_recv()
            total = total + x_in[k, d].astype(F32)
        gate, up = total[:, :cn], total[:, cn:]
        hid[k, f] = (gate / (1.0 + jnp.exp(-gate)) * up).astype(BF16)
        each(X - 1, lambda d: hx_copy(k, d).start())
        hp_copy(k).start()

    def forward(k):
        def step(d):
            hx_copy(k, d).wait_recv()
            hf_copy(k, d).start()

        each(X - 1, step)

    def arrived(k):
        hp_copy(k).wait_recv()
        each(X - 1, lambda d: hf_copy(k, d).wait_recv())
        wd_copy(k).wait()

    def product(k, j, n):
        lhs = hid[k, j * ob:(j + 1) * ob].reshape(block, cn)
        got = jnp.dot(lhs, wd[k, :, n * dn:(n + 1) * dn], preferred_element_type=F32)
        return acc[j * block:(j + 1) * block, n * dn:(n + 1) * dn] + got

    def accumulate(k):
        arrived(k)
        for j in range(rows // block):
            for n in range(nd):
                acc[j * block:(j + 1) * block, n * dn:(n + 1) * dn] = product(k, j, n)

    stages = (
        (0, nch, multiply), (1, nch, across), (X_LAG, nch, activate),
        (H_LAG, nch, forward), (D_LAG, nch - 1, accumulate),
    )

    def turn(t, _):
        for lag, count, stage in stages:
            k = t - lag

            @pl.when(jnp.logical_and(k >= 0, k < count))
            def _():
                stage(k)

        return 0

    lax.fori_loop(0, max(lag + count for lag, count, _ in stages), turn, 0)

    arrived(nch - 1)
    held = block // r_in
    for n in range(nd):
        for j in range(rows // block):
            got = product(nch - 1, j, n).astype(BF16)
            o_part[n, j * held:(j + 1) * held] = got.reshape(held, r_in, dn)
        each(H - 1, lambda d: o_copy(n, d).start())

    for n in range(nd):
        each(H - 1, lambda d: o_copy(n, d).wait_recv())
        total = o_part[n, h].astype(F32)
        for d in range(H - 1):
            total = total + o_in[n, d].astype(F32)
        out_ref[:, n * dn:(n + 1) * dn] = total.astype(BF16)

    each(H - 1, lambda d: tok_copy(d).wait_send())

    def sent(k):
        pair_copy(k).wait_send()
        hp_copy(k).wait_send()

        def over(d):
            x_copy(k, d).wait_send()
            hx_copy(k, d).wait_send()
            hf_copy(k, d).wait_send()

        each(X - 1, over)

    each(nch, sent)
    each(nd, lambda n: each(H - 1, lambda d: o_copy(n, d).wait_send()))


def shards(H, F, tokens, gate_weight, up_weight, down_weight):
    r_in, k1 = tokens.shape
    n1 = gate_weight.shape[1]
    k2, n2 = down_weight.shape
    X = F // 2
    rf = r_in * H // F
    cn = min(512, n1)
    dn = min(2048, n2)
    nch, nd = n1 // cn, n2 // dn
    dma = lambda *dims: pltpu.SemaphoreType.DMA(dims)
    buf = lambda *dims: pltpu.VMEM(dims, BF16)
    return pl.pallas_call(
        functools.partial(kernel, H, X),
        out_shape=jax.ShapeDtypeStruct((r_in, n2), BF16),
        in_specs=[pl.BlockSpec(memory_space=pl.ANY)] * 4,
        out_specs=pl.BlockSpec(memory_space=pltpu.VMEM),
        scratch_shapes=[
            buf(H, r_in, k1),
            buf(nch, k1, cn), buf(nch, k1, cn), buf(nch, cn, n2),
            buf(nch, X, 2, rf, 2 * cn), buf(nch, X, rf, 2 * cn),
            buf(nch, X - 1, rf, 2 * cn), buf(nch, X - 1, rf, 2 * cn),
            buf(nch, F, rf, cn),
            pltpu.VMEM((r_in * H, n2), F32),
            buf(nd, H, r_in, dn), buf(nd, H - 1, r_in, dn),
            dma(nch), dma(nch), dma(nch), pltpu.SemaphoreType.DMA,
            dma(H - 1), dma(H - 1),
            dma(nch), dma(nch), dma(nch, X - 1), dma(nch, X - 1),
            dma(nch), dma(nch), dma(nch, X - 1), dma(nch, X - 1),
            dma(nch, X - 1), dma(nch, X - 1),
            dma(nd, H - 1), dma(nd, H - 1),
        ],
        compiler_params=pltpu.CompilerParams(
            collective_id=0, has_side_effects=True, vmem_limit_bytes=60 * 2**20),
    )(tokens, gate_weight, up_weight, down_weight)


def solution(mesh):
    placed = (P(("grp", "hid"), "feat"), P("feat", "hid"), P("feat", "hid"), P("hid", "feat"))
    return jax.shard_map(
        functools.partial(shards, mesh.shape["hid"], mesh.shape["feat"]),
        mesh=mesh, in_specs=placed, out_specs=P(("grp", "hid"), "feat"), check_vma=False,
    )
```

```python
import functools

import jax
import jax.numpy as jnp
from jax import lax
from jax.experimental import pallas as pl
from jax.experimental.pallas import tpu as pltpu
from jax.sharding import PartitionSpec as P

MESH = pl.DeviceIdType.MESH
F32, BF16 = jnp.float32, jnp.bfloat16
X_LAG, H_LAG, D_LAG = 4, 6, 7


def each(count, body):
    if count <= 4:
        for i in range(count):
            body(i)
    else:
        lax.fori_loop(0, count, lambda i, _: (body(i), 0)[1], 0)


def kernel(
    H, X, tok_ref, gate_ref, up_ref, down_ref, out_ref,
    tok, wg, wu, wd, part, pair_in, x_out, x_in, hid, acc, o_part, o_in,
    wg_sem, wu_sem, wd_sem, own_sem, tok_s, tok_r, pair_s, pair_r, x_s, x_r,
    hp_s, hp_r, hx_s, hx_r, hf_s, hf_r, o_s, o_r,
):
    nch, _, cn = wg.shape
    nd, _, _, dn = o_part.shape
    F = 2 * X
    rf = part.shape[3]
    r_in = tok.shape[1]
    rows = H * r_in
    ob = max(2, min(F, 256 // rf))
    block = ob * rf

    h = lax.axis_index("hid")
    f = lax.axis_index("feat")
    x, c = lax.div(f, 2), lax.rem(f, 2)
    pair = {"feat": x * 2 + 1 - c}

    def x_peer(d):
        return lax.rem(x + d, X)

    def remote(src, dst, ssem, rsem, device):
        return pltpu.make_async_remote_copy(
            src_ref=src, dst_ref=dst, send_sem=ssem, recv_sem=rsem,
            device_id=device, device_id_type=MESH,
        )

    def cols(ref, k, n):
        return ref.at[:, pl.ds(pl.multiple_of(k * n, n), n)]

    def wg_copy(k):
        return pltpu.make_async_copy(cols(gate_ref, k, cn), wg.at[k], wg_sem.at[k])

    def wu_copy(k):
        return pltpu.make_async_copy(cols(up_ref, k, cn), wu.at[k], wu_sem.at[k])

    def wd_copy(k):
        rows_k = pl.ds(pl.multiple_of(k * cn, cn), cn)
        return pltpu.make_async_copy(down_ref.at[rows_k], wd.at[k], wd_sem.at[k])

    def tok_copy(d):
        to = lax.rem(h + d + 1, H)
        return remote(tok_ref, tok.at[h], tok_s.at[d], tok_r.at[d], {"hid": to})

    def pair_copy(k):
        return remote(part.at[k, :, 1 - c], pair_in.at[k], pair_s.at[k], pair_r.at[k], pair)

    def x_copy(k, d):
        to = {"feat": x_peer(d + 1) * 2 + c}
        return remote(x_out.at[k, d], x_in.at[k, d], x_s.at[k, d], x_r.at[k, d], to)

    def hp_copy(k):
        return remote(hid.at[k, f], hid.at[k, f], hp_s.at[k], hp_r.at[k], pair)

    def hx_copy(k, d):
        to = {"feat": x_peer(d + 1) * 2 + c}
        return remote(hid.at[k, f], hid.at[k, f], hx_s.at[k, d], hx_r.at[k, d], to)

    def hf_copy(k, d):
        owner = lax.rem(x + X - d - 1, X) * 2 + c
        piece = hid.at[k, owner]
        return remote(piece, piece, hf_s.at[k, d], hf_r.at[k, d], pair)

    def o_copy(n, d):
        to = lax.rem(h + d + 1, H)
        return remote(o_part.at[n, to], o_in.at[n, d], o_s.at[n, d], o_r.at[n, d], {"hid": to})

    own_copy = pltpu.make_async_copy(tok_ref, tok.at[h], own_sem)
    own_copy.start()

    barrier = pltpu.get_barrier_semaphore()
    each(H - 1, lambda d: pl.semaphore_signal(
        barrier, inc=1, device_id={"hid": lax.rem(h + d + 1, H)}, device_id_type=MESH))
    each(X - 1, lambda d: pl.semaphore_signal(
        barrier, inc=1, device_id={"feat": x_peer(d + 1) * 2 + c}, device_id_type=MESH))
    pl.semaphore_signal(barrier, inc=1, device_id=pair, device_id_type=MESH)

    def start_gate_up(k):
        wg_copy(k).start()
        wu_copy(k).start()

    each(nch, start_gate_up)
    each(nch, lambda k: wd_copy(k).start())
    acc[...] = jnp.zeros_like(acc)
    pl.semaphore_wait(barrier, H - 1 + X)

    each(H - 1, lambda d: tok_copy(d).start())
    own_copy.wait()
    each(H - 1, lambda d: tok_copy(d).wait_recv())

    def multiply(k):
        wg_copy(k).wait()
        wu_copy(k).wait()
        for j in range(rows // block):
            held = block // r_in
            lhs = tok[j * held:(j + 1) * held].reshape(block, tok.shape[2])
            for w, base in ((wg, 0), (wu, cn)):
                got = jnp.dot(lhs, w[k], preferred_element_type=F32).astype(BF16)
                got = got.reshape(ob // 2, 2, rf, cn)
                part[k, j * (ob // 2):(j + 1) * (ob // 2), :, :, base:base + cn] = got
        pair_copy(k).start()

    def across(k):
        pair_copy(k).wait_recv()

        def send(d):
            to = x_peer(d + 1)
            summed = part[k, to, c].astype(F32) + pair_in[k, to].astype(F32)
            x_out[k, d] = summed.astype(BF16)
            x_copy(k, d).start()

        each(X - 1, send)

    def activate(k):
        total = part[k, x, c].astype(F32) + pair_in[k, x].astype(F32)
        for d in range(X - 1):
            x_copy(k, d).wait_recv()
            total = total + x_in[k, d].astype(F32)
        gate, up = total[:, :cn], total[:, cn:]
        hid[k, f] = (gate / (1.0 + jnp.exp(-gate)) * up).astype(BF16)
        each(X - 1, lambda d: hx_copy(k, d).start())
        hp_copy(k).start()

    def forward(k):
        def step(d):
            hx_copy(k, d).wait_recv()
            hf_copy(k, d).start()

        each(X - 1, step)

    def arrived(k):
        hp_copy(k).wait_recv()
        each(X - 1, lambda d: hf_copy(k, d).wait_recv())
        wd_copy(k).wait()

    def product(k, j, n):
        lhs = hid[k, j * ob:(j + 1) * ob].reshape(block, cn)
        got = jnp.dot(lhs, wd[k, :, n * dn:(n + 1) * dn], preferred_element_type=F32)
        return acc[j * block:(j + 1) * block, n * dn:(n + 1) * dn] + got

    def accumulate(k):
        arrived(k)
        for j in range(rows // block):
            for n in range(nd):
                acc[j * block:(j + 1) * block, n * dn:(n + 1) * dn] = product(k, j, n)

    stages = (
        (0, nch, multiply), (1, nch, across), (X_LAG, nch, activate),
        (H_LAG, nch, forward), (D_LAG, nch - 1, accumulate),
    )

    def turn(t, _):
        for lag, count, stage in stages:
            k = t - lag

            @pl.when(jnp.logical_and(k >= 0, k < count))
            def _():
                stage(k)

        return 0

    lax.fori_loop(0, max(lag + count for lag, count, _ in stages), turn, 0)

    arrived(nch - 1)
    held = block // r_in
    for n in range(nd):
        for j in range(rows // block):
            got = product(nch - 1, j, n).astype(BF16)
            o_part[n, j * held:(j + 1) * held] = got.reshape(held, r_in, dn)
        each(H - 1, lambda d: o_copy(n, d).start())

    for n in range(nd):
        each(H - 1, lambda d: o_copy(n, d).wait_recv())
        total = o_part[n, h].astype(F32)
        for d in range(H - 1):
            total = total + o_in[n, d].astype(F32)
        out_ref[:, n * dn:(n + 1) * dn] = total.astype(BF16)

    each(H - 1, lambda d: tok_copy(d).wait_send())

    def sent(k):
        pair_copy(k).wait_send()
        hp_copy(k).wait_send()

        def over(d):
            x_copy(k, d).wait_send()
            hx_copy(k, d).wait_send()
            hf_copy(k, d).wait_send()

        each(X - 1, over)

    each(nch, sent)
    each(nd, lambda n: each(H - 1, lambda d: o_copy(n, d).wait_send()))


def shards(H, F, tokens, gate_weight, up_weight, down_weight):
    r_in, k1 = tokens.shape
    n1 = gate_weight.shape[1]
    k2, n2 = down_weight.shape
    X = F // 2
    rf = r_in * H // F
    cn = min(512, n1)
    dn = min(2048, n2)
    nch, nd = n1 // cn, n2 // dn
    dma = lambda *dims: pltpu.SemaphoreType.DMA(dims)
    buf = lambda *dims: pltpu.VMEM(dims, BF16)
    return pl.pallas_call(
        functools.partial(kernel, H, X),
        out_shape=jax.ShapeDtypeStruct((r_in, n2), BF16),
        in_specs=[pl.BlockSpec(memory_space=pl.ANY)] * 4,
        out_specs=pl.BlockSpec(memory_space=pltpu.VMEM),
        scratch_shapes=[
            buf(H, r_in, k1),
            buf(nch, k1, cn), buf(nch, k1, cn), buf(nch, cn, n2),
            buf(nch, X, 2, rf, 2 * cn), buf(nch, X, rf, 2 * cn),
            buf(nch, X - 1, rf, 2 * cn), buf(nch, X - 1, rf, 2 * cn),
            buf(nch, F, rf, cn),
            pltpu.VMEM((r_in * H, n2), F32),
            buf(nd, H, r_in, dn), buf(nd, H - 1, r_in, dn),
            dma(nch), dma(nch), dma(nch), pltpu.SemaphoreType.DMA,
            dma(H - 1), dma(H - 1),
            dma(nch), dma(nch), dma(nch, X - 1), dma(nch, X - 1),
            dma(nch), dma(nch), dma(nch, X - 1), dma(nch, X - 1),
            dma(nch, X - 1), dma(nch, X - 1),
            dma(nd, H - 1), dma(nd, H - 1),
        ],
        compiler_params=pltpu.CompilerParams(
            collective_id=0, has_side_effects=True, vmem_limit_bytes=60 * 2**20),
    )(tokens, gate_weight, up_weight, down_weight)


def solution(mesh):
    placed = (P(("grp", "hid"), "feat"), P("feat", "hid"), P("feat", "hid"), P("hid", "feat"))
    return jax.shard_map(
        functools.partial(shards, mesh.shape["hid"], mesh.shape["feat"]),
        mesh=mesh, in_specs=placed, out_specs=P(("grp", "hid"), "feat"), check_vma=False,
    )
```
